32 devices in a mesh: sec: 2 (over x), blk: 8 (over z, y), head: 2 (over core).
Axes of the slice: x: 2, y: 2, z: 4, core: 2. Of those that a mesh axis runs over, the one named last changes fastest.
Arguments:
- tokens: bfloat16 [8192, 768], P(('sec', 'blk')), parts along dimension 0, may hold values from -6 to 6
- counts: int32 [16], P(('sec', 'blk')), parts along dimension 0, may hold values from 128 to 512, as said below
- face_owner: int32 [6, 8192], P(None, ('sec', 'blk')), parts along dimension 1, may hold values from 0 to 7, as said below
- face_row: int32 [6, 8192], P(None, ('sec', 'blk')), parts along dimension 1, may hold values from 0 to 511, as said below
- face_count: int32 [8192], P(('sec', 'blk')), parts along dimension 0, may hold values from 1 to 6
- mix_weight: bfloat16 [768, 768], P(None, 'head'), may hold values from -0.21875 to 0.21875
- norm_gain: bfloat16 [768], replicated, may hold values from 0.25 to 1.75
- query_weight: bfloat16 [768, 768], P(None, 'head'), may hold values from -1 to 1
- key_weight: bfloat16 [768, 768], P(None, 'head'), may hold values from -1 to 1
- value_weight: bfloat16 [768, 768], P(None, 'head'), may hold values from -0.21875 to 0.21875
- out_weight: bfloat16 [768, 768], P('head'), may hold values from -0.21875 to 0.21875
Outputs:
- layer_out: bfloat16 [8192, 768], P(('sec', 'blk'), 'head'), parts along dimension 0
The draws below stay inside these ranges and needn't reach their ends.
There are 2 independent parts, one for each index of `sec`. The reference program is written for one: setup_inputs(seed, part) draws one part's arguments, and reference() takes and returns one part's arrays. A program takes and returns all parts, laid end to end along the dimension named above; an argument that names none is the same for every part. Nothing has to cross between parts.
Inputs may be any that keep to these rules, and one draw needn't show every extreme that they name: `counts`: each section has one block with exactly 512 live tokens and one with exactly 128. `face_owner`: A token's face neighbours lie in its own block or in the blocks one index below or above it, the last block's above being block 0. `face_row`: A face neighbour is a live slot of its owner's block.
All inputs are finite; a program needn't handle non-finite values.
Results may differ from the reference program's by a relative error of at most 0.012.
The reference program's roundings to bfloat16 on the way (of `summed`, `stream`, `normed`, `weight` and `context`) count: a program that leaves them out, or rounds other values in their place, can miss the bound.
Values may be sent and summed in bfloat16 or wider, within the bound.
A program may use at most 64 MiB of HBM per device.

```python
import jax
import jax.numpy as jnp
from jax import lax

D = 768
NH = 12
HS = 64
FACES = 6
TOK_DEV = 512
CYCLE = 8
TOKENS = 4096


def section_counts(key):
    base = jax.random.randint(jax.random.fold_in(key, 11), (CYCLE,), TOK_DEV // 4, TOK_DEV + 1)
    fullest = jax.random.randint(jax.random.fold_in(key, 12), (), 0, CYCLE)
    step = jax.random.randint(jax.random.fold_in(key, 13), (), 1, CYCLE)
    emptiest = (fullest + step) % CYCLE
    index = jnp.arange(CYCLE, dtype=jnp.int32)
    base = jnp.where(index == fullest, TOK_DEV, base)
    base = jnp.where(index == emptiest, TOK_DEV // 4, base)
    return base.astype(jnp.int32)


def face_table(key):
    live_counts = section_counts(key)
    home = jnp.arange(TOKENS, dtype=jnp.int32) // TOK_DEV
    offset = jax.random.randint(jax.random.fold_in(key, 21), (FACES, TOKENS), -1, 2)
    owner = (home[None, :] + offset + CYCLE) % CYCLE
    limit = live_counts[owner]
    raw = jax.random.randint(jax.random.fold_in(key, 22), (FACES, TOKENS), 0, TOK_DEV)
    return (owner.astype(jnp.int32), (raw % limit).astype(jnp.int32))


def attention_weight(key, which):
    base = jax.random.normal(jax.random.fold_in(key, 41 + which), (D, D), jnp.float32)
    base = jnp.clip(base, -6.0, 6.0) / D ** 0.5
    return jnp.clip(base, -1.0, 1.0)


def draw_counts(key, part):
    return section_counts(key)


def draw_face_owner(key, part):
    return face_table(key)[0]


def draw_face_row(key, part):
    return face_table(key)[1]


def draw_face_count(key, part):
    return jax.random.randint(jax.random.fold_in(key, 31), (TOKENS,), 1, FACES + 1).astype(jnp.int32)


def draw_query_weight(key, part):
    return attention_weight(key, 0).astype(jnp.bfloat16)


def draw_key_weight(key, part):
    return attention_weight(key, 1).astype(jnp.bfloat16)


def levels(own_key, dims, split, low, high):
    level, own = 1.0, jax.random.fold_in(own_key, 6)
    for dim, parts in split:
        steps = jnp.exp(jax.random.uniform(jax.random.fold_in(own, dim), (parts,), jnp.float32, low / len(split), high / len(split)))
        level = level * jnp.repeat(steps, dims[dim] // parts).reshape([-1 if axis == dim else 1 for axis in range(len(dims))])
    return level


def normal_values(own_key, extent, deviation, reach, shards=(), kind=jnp.bfloat16):
    values = jax.random.normal(own_key, extent, jnp.float32) * deviation
    if len(shards) > 0:
        values = levels(own_key, extent, shards, -0.22, 0.18) * values
    return jnp.clip(values, min=-reach, max=reach).astype(kind)


def setup_inputs(seed: int = 0, part: int = 0) -> dict:
    key_list = jax.random.split(jax.random.key(seed), 12)
    own_keys = jax.random.split(jax.random.fold_in(key_list[11], part), 12)
    return {
        "tokens": normal_values(own_keys[0], (TOKENS, D), 1.0, 6.0, ((0, 8),)),
        "counts": draw_counts(jax.random.fold_in(jax.random.fold_in(key_list[11], part), 71), part),
        "face_owner": draw_face_owner(jax.random.fold_in(jax.random.fold_in(key_list[11], part), 71), part),
        "face_row": draw_face_row(jax.random.fold_in(jax.random.fold_in(key_list[11], part), 71), part),
        "face_count": draw_face_count(jax.random.fold_in(jax.random.fold_in(key_list[11], part), 71), part),
        "mix_weight": normal_values(key_list[5], (D, D), D ** -0.5, 0.21875, ((1, 2),)),
        "norm_gain": jnp.clip(1.0 + 0.15 * jax.random.normal(key_list[6], (D,), jnp.float32), 0.25, 1.75).astype(jnp.bfloat16),
        "query_weight": draw_query_weight(jax.random.fold_in(key_list[11], 71), part),
        "key_weight": draw_key_weight(jax.random.fold_in(key_list[11], 71), part),
        "value_weight": normal_values(key_list[9], (D, D), D ** -0.5, 0.21875, ((1, 2),)),
        "out_weight": normal_values(key_list[10], (D, D), D ** -0.5, 0.21875, ((0, 2),)),
    }


def rms_norm(values, gain):
    var = lax.optimization_barrier(jnp.mean(values * values, axis=-1, keepdims=True))
    return values * lax.rsqrt(var + 1e-05) * gain

def reference(tokens, counts, face_owner, face_row, face_count, mix_weight, norm_gain, query_weight, key_weight, value_weight, out_weight):
    total = tokens.shape[0]
    flat_index = (face_owner * TOK_DEV + face_row).astype(jnp.int32)
    picked = tokens.astype(jnp.float32)[flat_index]
    live = jnp.arange(FACES, dtype=jnp.int32)[:, None] < face_count[None, :]
    summed = lax.optimization_barrier(jnp.sum(jnp.where(live[:, :, None], picked, 0.0), axis=0))
    summed = (summed / face_count[:, None].astype(jnp.float32)).astype(jnp.bfloat16)
    stream = (tokens.astype(jnp.float32) + jnp.dot(summed, mix_weight, preferred_element_type=jnp.float32)).astype(jnp.bfloat16)
    normed = rms_norm(stream.astype(jnp.float32), norm_gain.astype(jnp.float32)).astype(jnp.bfloat16)
    query = jnp.dot(normed, query_weight, preferred_element_type=jnp.float32).astype(jnp.bfloat16)
    key = jnp.dot(normed, key_weight, preferred_element_type=jnp.float32).astype(jnp.bfloat16)
    value = jnp.dot(normed, value_weight, preferred_element_type=jnp.float32).astype(jnp.bfloat16)
    key_live = (jnp.arange(TOK_DEV, dtype=jnp.int32)[None, :] < counts[:, None]).reshape(-1)
    scale = 1.0 / HS ** 0.5

    def split_heads(values):
        return values.astype(jnp.float32).reshape(total, NH, HS).transpose(1, 0, 2)

    def one_head(operands):
        query_head, key_head, value_head = operands

        def one_block(query_block):
            scores = jnp.dot(query_block, key_head.T) * scale
            scores = jnp.where(key_live[None, :], scores, -1e+30)
            top = lax.optimization_barrier(jnp.max(scores, axis=-1, keepdims=True))
            probs = jnp.where(key_live[None, :], jnp.exp(scores - top), 0.0)
            weight = probs.astype(jnp.bfloat16).astype(jnp.float32)
            return jnp.dot(weight, value_head) / lax.optimization_barrier(jnp.sum(probs, axis=-1, keepdims=True))
        blocks = lax.map(one_block, query_head.reshape(total // TOK_DEV, TOK_DEV, HS))
        return blocks.reshape(total, HS)
    context = lax.map(one_head, (split_heads(query), split_heads(key), split_heads(value)))
    context = context.transpose(1, 0, 2).reshape(total, D).astype(jnp.bfloat16)
    result = stream.astype(jnp.float32) + jnp.dot(context, out_weight, preferred_element_type=jnp.float32)
    return result.astype(jnp.bfloat16)
```

```python
import functools
import math

import jax
import jax.numpy as jnp
from jax import lax
from jax.experimental import pallas as pl
from jax.experimental.pallas import tpu as pltpu
from jax.sharding import PartitionSpec as P

MESH = pl.DeviceIdType.MESH
HS = 64
NT = (((1,), (1,)), ((), ()))
F32 = jnp.float32
BF16 = jnp.bfloat16


def kernel(
    n, lanes_y,
    tokens, counts, face_owner, face_row, face_count, gain, mix_w, query_w, key_w, value_w, out_w,
    out,
    ext, own_rows, onehot, pack, summed, all_normed, stream_half, count_all,
    mix_full, wq, wk, wv, wvt, wo, qm, vt, acc, top, sent_out, got_out, own_out,
    local_sem, halo_send, halo_recv, mix_sem, sum_sem, count_send, count_recv,
    z_send, z_recv, y_send, y_recv, sib_send, sib_recv, stream_sem, out_sem,
):
    rows, width = tokens.shape
    half_w = width // 2
    half_r = rows // 2
    heads = half_w // HS
    faces = face_owner.shape[0]
    b = lax.axis_index("blk")
    c = lax.axis_index("head")
    other = 1 - c
    nz = n // lanes_y
    zi, yi = b // lanes_y, b % lanes_y
    my_rows = pl.ds(pl.multiple_of(c * half_r, half_r), half_r)
    sib_rows = pl.ds(pl.multiple_of(other * half_r, half_r), half_r)
    my_cols = pl.ds(pl.multiple_of(c * half_w, 128), half_w)
    sib_cols = pl.ds(pl.multiple_of(other * half_w, 128), half_w)

    def remote(src, dst, send, recv, **where):
        return pltpu.make_async_remote_copy(
            src_ref=src, dst_ref=dst, send_sem=send, recv_sem=recv,
            device_id=where, device_id_type=MESH,
        )

    loads = [
        pltpu.make_async_copy(tokens.at[:, my_cols], ext.at[1], local_sem.at[0]),
        pltpu.make_async_copy(tokens.at[my_rows, :], own_rows, local_sem.at[1]),
        pltpu.make_async_copy(mix_w, mix_full.at[:, my_cols], local_sem.at[2]),
        pltpu.make_async_copy(query_w, wq, local_sem.at[3]),
        pltpu.make_async_copy(key_w, wk, local_sem.at[4]),
        pltpu.make_async_copy(value_w, wv, local_sem.at[5]),
        pltpu.make_async_copy(out_w, wo, local_sem.at[6]),
    ]

    barrier = pltpu.get_barrier_semaphore()
    for j in range(1, n):
        pl.semaphore_signal(barrier, inc=1, device_id={"blk": (b + j) % n}, device_id_type=MESH)
    pl.semaphore_signal(barrier, inc=1, device_id={"head": other}, device_id_type=MESH)
    pl.semaphore_wait(barrier, n)

    up, down = (b + 1) % n, (b + n - 1) % n
    halo_up = remote(tokens.at[:, my_cols], ext.at[0], halo_send.at[0], halo_recv.at[0], blk=up)
    halo_down = remote(tokens.at[:, my_cols], ext.at[2], halo_send.at[1], halo_recv.at[1], blk=down)
    halo_up.start()
    halo_down.start()
    mix_copy = remote(mix_w, mix_full.at[:, my_cols], mix_sem.at[0], mix_sem.at[1], head=other)
    mix_copy.start()
    for load in loads:
        load.start()

    count_all[b] = jnp.full((8, 128), counts[0], jnp.int32)

    def count_copy(j):
        return remote(
            count_all.at[b], count_all.at[b], count_send.at[j], count_recv.at[j], blk=(b + j) % n
        )

    for j in range(1, n):
        count_copy(j).start()

    off = face_owner[...] - b + 1
    off = jnp.where(off < 0, off + n, off)
    off = jnp.where(off >= n, off - n, off)
    index = off * rows + face_row[...]
    face = lax.broadcasted_iota(jnp.int32, (faces, rows), 0)
    index = jnp.where(face < face_count[...], index, -1)
    pack[...] = jnp.zeros_like(pack)
    pack[0:faces, :] = index.astype(F32)
    pack[faces : faces + 1, :] = face_count[...].astype(F32)
    pack_t = pack[...].T
    face_total = pack_t[:, faces : faces + 1]
    for s in range(3):
        place = (lax.broadcasted_iota(jnp.int32, (rows, rows), 1) + s * rows).astype(F32)
        total = jnp.zeros((rows, rows), F32)
        for f in range(faces):
            total = total + jnp.where(pack_t[:, f : f + 1] == place, 1.0, 0.0)
        onehot[:, s * rows : (s + 1) * rows] = total.astype(BF16)

    for load in loads:
        load.wait()
    wvt[...] = wv[...].astype(F32).T.astype(BF16)
    acc[...] = jnp.zeros_like(acc)
    top[...] = jnp.full_like(top, -1e30)

    part = jnp.dot(onehot[:, rows : 2 * rows], ext[1], preferred_element_type=F32)
    halo_up.wait()
    part += jnp.dot(onehot[:, 0:rows], ext[0], preferred_element_type=F32)
    halo_down.wait()
    part += jnp.dot(onehot[:, 2 * rows :], ext[2], preferred_element_type=F32)
    summed[:, my_cols] = (part / face_total).astype(BF16)
    sum_copy = remote(
        summed.at[sib_rows, my_cols], summed.at[sib_rows, my_cols], sum_sem.at[0], sum_sem.at[1],
        head=other,
    )
    sum_copy.start()
    mix_copy.wait()
    sum_copy.wait()
    stream = own_rows[...].astype(F32) + jnp.dot(
        summed[my_rows, :], mix_full[...], preferred_element_type=F32
    )
    own_rows[...] = stream.astype(BF16)
    stream = own_rows[...].astype(F32)
    var = jnp.mean(stream * stream, axis=-1, keepdims=True)
    all_normed[b, my_rows, :] = (stream * lax.rsqrt(var + 1e-05) * gain[...].astype(F32)).astype(
        BF16
    )

    def half(block):
        return all_normed.at[block, my_rows]

    def z_copy(block, direction):
        step = 2 * direction - 1
        return remote(
            half(block), half(block), z_send.at[direction, block // lanes_y],
            z_recv.at[block // lanes_y], blk=b + step * lanes_y,
        )

    def y_copy(block):
        return remote(
            half(block), half(block), y_send.at[block // lanes_y], y_recv.at[block // lanes_y],
            blk=zi * lanes_y + (lanes_y - 1 - yi),
        )

    def sib_copy(block):
        return remote(
            half(block), half(block), sib_send.at[block], sib_recv.at[block], head=other
        )

    def sib_arrival(block):
        return remote(
            all_normed.at[block, sib_rows], all_normed.at[block, sib_rows],
            sib_send.at[block], sib_recv.at[block], head=other,
        )

    near = jnp.minimum(zi, nz - 1 - zi)
    far_sign = jnp.where(zi < nz - 1 - zi, 1, -1)

    def line(k):
        close = zi + (1 - 2 * (k % 2)) * ((k + 1) // 2)
        return jnp.where(k <= 2 * near, close, zi + far_sign * (k - near))

    def on_line(k):
        z = line(k)
        block = z * lanes_y + yi

        @pl.when(k > 0)
        def _():
            z_copy(block, 1).wait_recv()

        @pl.when((z <= zi) & (zi < nz - 1))
        def _():
            z_copy(block, 1).start()

        @pl.when((z >= zi) & (zi > 0))
        def _():
            z_copy(block, 0).start()

        if lanes_y > 1:
            y_copy(block).start()
        sib_copy(block).start()
        return block

    def across(k):
        block = line(k) * lanes_y + (lanes_y - 1 - yi)
        y_copy(block).wait_recv()
        sib_copy(block).start()
        return block

    def attend(block):
        live = count_all[block]
        normed = all_normed[block]
        live_row = lax.broadcasted_iota(jnp.int32, (rows, half_w), 0) < live[0:1, 0:1]
        keys = jnp.dot(normed, wk[...], preferred_element_type=F32)
        keys = jnp.where(live_row, keys, keys[0:1, :]).astype(BF16)
        live_col = lax.broadcasted_iota(jnp.int32, (half_w, rows), 1) < live[0:1, 0:1]
        values = lax.dot_general(wvt[...], normed, NT, preferred_element_type=F32)
        values = jnp.where(live_col, values, 0.0).astype(BF16)
        ones = jnp.where(live_col[0:16, :], 1.0, 0.0).astype(BF16)
        for h in range(heads):
            pair = (h // 2) * 2 * HS
            vt[h, 0:HS, :] = values[h * HS : (h + 1) * HS, :]
            vt[h, HS:, :] = ones
            scores = lax.dot_general(
                keys[:, pair : pair + 2 * HS], qm[h], NT, preferred_element_type=F32
            )
            old = top[h : h + 1, :]
            new = jnp.maximum(old, jnp.max(scores, axis=0, keepdims=True))
            probs = jnp.exp2(scores - new).astype(BF16)
            top[h : h + 1, :] = new
            acc[h] = acc[h] * jnp.exp2(old - new) + jnp.dot(
                vt[h], probs, preferred_element_type=F32
            )

    on_line(0)
    stream_half[my_rows, :] = own_rows[:, my_cols]
    stream_copy = remote(
        own_rows.at[:, sib_cols], stream_half.at[my_rows], stream_sem.at[0], stream_sem.at[1],
        head=other,
    )
    stream_copy.start()
    for j in range(1, n):
        count_copy(j).wait()
    sib_arrival(b).wait_recv()
    query = jnp.dot(all_normed[b], wq[...], preferred_element_type=F32) * (
        math.log2(math.e) / HS**0.5
    )
    lane = lax.broadcasted_iota(jnp.int32, (rows, 2 * HS), 1) // HS
    for h in range(heads):
        pair = (h // 2) * 2 * HS
        qm[h] = jnp.where(lane == h % 2, query[:, pair : pair + 2 * HS], 0.0).astype(BF16)

    attend(b)

    if lanes_y > 1:

        def step(i, carry):
            is_line = (i % 2 == 1) & (i < n - 1)
            k = jnp.where(is_line, (i + 1) // 2, i // 2 - 1 + (i // (n - 1)) * (nz - 1 - (i // 2 - 1)))

            @pl.when(is_line)
            def _():
                on_line(k)

            @pl.when(jnp.logical_not(is_line))
            def _():
                across(k)

            block = line(k) * lanes_y + jnp.where(is_line, yi, lanes_y - 1 - yi)
            sib_arrival(block).wait_recv()
            attend(block)
            return carry

    else:

        def step(i, carry):
            block = on_line(i)
            sib_arrival(block).wait_recv()
            attend(block)
            return carry

    lax.fori_loop(1, n, step, 0)

    context = []
    for h in range(heads):
        context.append(acc[h, 0:HS, :] / acc[h, HS : HS + 1, :])
    context = jnp.concatenate(context, axis=0).T.astype(BF16)
    sent_out[...] = jnp.dot(context, wo[:, sib_cols], preferred_element_type=F32).astype(BF16)
    out_copy = remote(sent_out, got_out, out_sem.at[0], out_sem.at[1], head=other)
    out_copy.start()
    mine = jnp.dot(context, wo[:, my_cols], preferred_element_type=F32)
    stream_copy.wait()
    mine = mine + stream_half[...].astype(F32)
    out_copy.wait()
    out[...] = (mine + got_out[...].astype(F32)).astype(BF16)

    def drain(k, carry):
        z = line(k)
        block = z * lanes_y + yi

        @pl.when((z <= zi) & (zi < nz - 1))
        def _():
            z_copy(block, 1).wait_send()

        @pl.when((z >= zi) & (zi > 0))
        def _():
            z_copy(block, 0).wait_send()

        if lanes_y > 1:
            y_copy(block).wait_send()
            sib_copy(z * lanes_y + (lanes_y - 1 - yi)).wait_send()
        sib_copy(block).wait_send()
        return carry

    lax.fori_loop(0, nz, drain, 0)


def local(n, lanes_y, tokens, counts, face_owner, face_row, face_count, mix_w, gain, query_w, key_w, value_w, out_w):
    rows, width = tokens.shape
    half_w = width // 2
    heads = half_w // HS
    nz = n // lanes_y
    any_, vmem = pl.BlockSpec(memory_space=pl.ANY), pl.BlockSpec(memory_space=pltpu.VMEM)
    smem = pl.BlockSpec(memory_space=pltpu.SMEM)
    sem = pltpu.SemaphoreType.DMA
    return pl.pallas_call(
        functools.partial(kernel, n, lanes_y),
        out_shape=jax.ShapeDtypeStruct((rows, half_w), BF16),
        in_specs=[any_, smem, vmem, vmem, vmem, vmem, any_, any_, any_, any_, any_],
        out_specs=vmem,
        scratch_shapes=[
            pltpu.VMEM((3, rows, half_w), BF16),
            pltpu.VMEM((rows // 2, width), BF16),
            pltpu.VMEM((rows, 3 * rows), BF16),
            pltpu.VMEM((128, rows), F32),
            pltpu.VMEM((rows, width), BF16),
            pltpu.VMEM((n, rows, width), BF16),
            pltpu.VMEM((rows, half_w), BF16),
            pltpu.VMEM((n, 8, 128), jnp.int32),
            pltpu.VMEM((width, width), BF16),
            pltpu.VMEM((width, half_w), BF16),
            pltpu.VMEM((width, half_w), BF16),
            pltpu.VMEM((width, half_w), BF16),
            pltpu.VMEM((half_w, width), BF16),
            pltpu.VMEM((half_w, width), BF16),
            pltpu.VMEM((heads, rows, 2 * HS), BF16),
            pltpu.VMEM((heads, HS + 16, rows), BF16),
            pltpu.VMEM((heads, HS + 16, rows), F32),
            pltpu.VMEM((8, rows), F32),
            pltpu.VMEM((rows, half_w), BF16),
            pltpu.VMEM((rows, half_w), BF16),
            pltpu.VMEM((rows, half_w), F32),
            sem((7,)), sem((2,)), sem((2,)), sem((2,)), sem((2,)), sem((n,)), sem((n,)),
            sem((2, nz)), sem((nz,)), sem((nz,)), sem((nz,)), sem((n,)), sem((n,)), sem((2,)), sem((2,)),
        ],
        compiler_params=pltpu.CompilerParams(
            collective_id=0, has_side_effects=True, vmem_limit_bytes=50 * 2**20
        ),
    )(
        tokens, counts, face_owner, face_row, face_count[None, :], gain[None, :],
        mix_w, query_w, key_w, value_w, out_w,
    )


def solution(mesh):
    n = mesh.shape["blk"]
    lanes_y = 2 if n == 8 else 1
    rows = P(("sec", "blk"), None)
    in_specs = (
        rows, P(("sec", "blk")), P(None, ("sec", "blk")), P(None, ("sec", "blk")),
        P(("sec", "blk")), P(None, "head"), P(), P(None, "head"), P(None, "head"),
        P(None, "head"), P("head", None),
    )
    return jax.shard_map(
        functools.partial(local, n, lanes_y), mesh=mesh, in_specs=in_specs,
        out_specs=P(("sec", "blk"), "head"), check_vma=False,
    )
```

```python
import functools
import math

import jax
import jax.numpy as jnp
from jax import lax
from jax.experimental import pallas as pl
from jax.experimental.pallas import tpu as pltpu
from jax.sharding import PartitionSpec as P

MESH = pl.DeviceIdType.MESH
HS = 64
NT = (((1,), (1,)), ((), ()))
F32 = jnp.float32
BF16 = jnp.bfloat16


def kernel(
    n, lanes_y,
    tokens, counts, face_owner, face_row, face_count, gain, mix_w, query_w, key_w, value_w, out_w,
    out,
    ext, own_rows, onehot, pack, summed, all_normed, stream_half, count_all,
    mix_full, wq, wk, wv, wvt, wo, qm, vt, acc, top, sent_out, got_out,
    local_sem, halo_send, halo_recv, mix_sem, sum_sem, count_send, count_recv,
    z_send, z_recv, y_send, y_recv, sib_send, sib_recv, stream_sem, out_sem,
):
    rows, width = tokens.shape
    half_w = width // 2
    half_r = rows // 2
    piece = half_r // 2
    heads = half_w // HS
    faces = face_owner.shape[0]
    b = lax.axis_index("blk")
    c = lax.axis_index("head")
    other = 1 - c
    nz = n // lanes_y
    zi, yi = b // lanes_y, b % lanes_y
    my_rows = pl.ds(pl.multiple_of(c * half_r, half_r), half_r)
    sib_rows = pl.ds(pl.multiple_of(other * half_r, half_r), half_r)
    my_cols = pl.ds(pl.multiple_of(c * half_w, 128), half_w)
    sib_cols = pl.ds(pl.multiple_of(other * half_w, 128), half_w)

    def remote(src, dst, send, recv, **where):
        return pltpu.make_async_remote_copy(
            src_ref=src, dst_ref=dst, send_sem=send, recv_sem=recv,
            device_id=where, device_id_type=MESH,
        )

    loads = [
        pltpu.make_async_copy(tokens.at[:, my_cols], ext.at[1], local_sem.at[0]),
        pltpu.make_async_copy(tokens.at[my_rows, :], own_rows, local_sem.at[1]),
        pltpu.make_async_copy(mix_w, mix_full.at[:, my_cols], local_sem.at[2]),
        pltpu.make_async_copy(query_w, wq, local_sem.at[3]),
        pltpu.make_async_copy(key_w, wk, local_sem.at[4]),
        pltpu.make_async_copy(value_w, wv, local_sem.at[5]),
        pltpu.make_async_copy(out_w, wo, local_sem.at[6]),
    ]

    barrier = pltpu.get_barrier_semaphore()
    for j in range(1, n):
        pl.semaphore_signal(barrier, inc=1, device_id={"blk": (b + j) % n}, device_id_type=MESH)
    pl.semaphore_signal(barrier, inc=1, device_id={"head": other}, device_id_type=MESH)
    pl.semaphore_wait(barrier, n)

    up, down = (b + 1) % n, (b + n - 1) % n
    halo_up = remote(tokens.at[:, my_cols], ext.at[0], halo_send.at[0], halo_recv.at[0], blk=up)
    halo_down = remote(tokens.at[:, my_cols], ext.at[2], halo_send.at[1], halo_recv.at[1], blk=down)
    halo_up.start()
    halo_down.start()
    mix_copy = remote(mix_w, mix_full.at[:, my_cols], mix_sem.at[0], mix_sem.at[1], head=other)
    mix_copy.start()
    for load in loads:
        load.start()

    count_all[b] = jnp.full((8, 128), counts[0], jnp.int32)

    def count_copy(j):
        return remote(
            count_all.at[b], count_all.at[b], count_send.at[j], count_recv.at[j], blk=(b + j) % n
        )

    for j in range(1, n):
        count_copy(j).start()

    off = face_owner[...] - b + 1
    off = jnp.where(off < 0, off + n, off)
    off = jnp.where(off >= n, off - n, off)
    index = off * rows + face_row[...]
    face = lax.broadcasted_iota(jnp.int32, (faces, rows), 0)
    index = jnp.where(face < face_count[...], index, -1)
    pack[...] = jnp.zeros_like(pack)
    pack[0:faces, :] = index.astype(F32)
    pack[faces : faces + 1, :] = face_count[...].astype(F32)
    pack_t = pack[...].T
    face_total = pack_t[:, faces : faces + 1]
    for s in range(3):
        place = (lax.broadcasted_iota(jnp.int32, (rows, rows), 1) + s * rows).astype(F32)
        total = jnp.zeros((rows, rows), F32)
        for f in range(faces):
            total = total + jnp.where(pack_t[:, f : f + 1] == place, 1.0, 0.0)
        onehot[:, s * rows : (s + 1) * rows] = total.astype(BF16)

    for load in loads:
        load.wait()
    wvt[...] = wv[...].astype(F32).T.astype(BF16)
    acc[...] = jnp.zeros_like(acc)
    top[...] = jnp.full_like(top, -1e30)

    part = jnp.dot(onehot[:, rows : 2 * rows], ext[1], preferred_element_type=F32)
    halo_up.wait()
    part += jnp.dot(onehot[:, 0:rows], ext[0], preferred_element_type=F32)
    halo_down.wait()
    part += jnp.dot(onehot[:, 2 * rows :], ext[2], preferred_element_type=F32)
    summed[:, my_cols] = (part / face_total).astype(BF16)
    sum_copy = remote(
        summed.at[sib_rows, my_cols], summed.at[sib_rows, my_cols], sum_sem.at[0], sum_sem.at[1],
        head=other,
    )
    sum_copy.start()
    mix_copy.wait()
    sum_copy.wait()
    stream = own_rows[...].astype(F32) + jnp.dot(
        summed[my_rows, :], mix_full[...], preferred_element_type=F32
    )
    own_rows[...] = stream.astype(BF16)
    stream = own_rows[...].astype(F32)
    var = jnp.mean(stream * stream, axis=-1, keepdims=True)
    all_normed[b, my_rows, :] = (stream * lax.rsqrt(var + 1e-05) * gain[...].astype(F32)).astype(
        BF16
    )

    def chunk(block, ch):
        return all_normed.at[block, pl.ds(pl.multiple_of(c * half_r + ch * piece, piece), piece)]

    def z_copy(block, ch, direction):
        step = 2 * direction - 1
        return remote(
            chunk(block, ch), chunk(block, ch), z_send.at[direction, block // lanes_y, ch],
            z_recv.at[block // lanes_y, ch], blk=b + step * lanes_y,
        )

    def y_copy(block, ch):
        return remote(
            chunk(block, ch), chunk(block, ch), y_send.at[block // lanes_y, ch],
            y_recv.at[block // lanes_y, ch], blk=zi * lanes_y + (lanes_y - 1 - yi),
        )

    def sib_copy(block, ch):
        return remote(
            chunk(block, ch), chunk(block, ch), sib_send.at[block, ch], sib_recv.at[block, ch],
            head=other,
        )

    def sib_arrival(block, ch):
        place = pl.ds(pl.multiple_of(other * half_r + ch * piece, piece), piece)
        return remote(
            all_normed.at[block, place], all_normed.at[block, place],
            sib_send.at[block, ch], sib_recv.at[block, ch], head=other,
        )

    near = jnp.minimum(zi, nz - 1 - zi)
    far_sign = jnp.where(zi < nz - 1 - zi, 1, -1)

    def line(k):
        close = zi + (1 - 2 * (k % 2)) * ((k + 1) // 2)
        return jnp.where(k <= 2 * near, close, zi + far_sign * (k - near))

    def on_line(k, ch, first=False):
        z = line(k)
        block = z * lanes_y + yi
        if not first:
            z_copy(block, ch, 1).wait_recv()

        @pl.when((z <= zi) & (zi < nz - 1))
        def _():
            z_copy(block, ch, 1).start()

        @pl.when((z >= zi) & (zi > 0))
        def _():
            z_copy(block, ch, 0).start()

        if lanes_y > 1:
            y_copy(block, ch).start()
        sib_copy(block, ch).start()

    def across(k, ch):
        block = line(k) * lanes_y + (lanes_y - 1 - yi)
        y_copy(block, ch).wait_recv()
        sib_copy(block, ch).start()

    def attend(block):
        live = count_all[block]
        normed = all_normed[block]
        live_row = lax.broadcasted_iota(jnp.int32, (rows, half_w), 0) < live[0:1, 0:1]
        keys = jnp.dot(normed, wk[...], preferred_element_type=F32)
        keys = jnp.where(live_row, keys, keys[0:1, :]).astype(BF16)
        live_col = lax.broadcasted_iota(jnp.int32, (half_w, rows), 1) < live[0:1, 0:1]
        values = lax.dot_general(wvt[...], normed, NT, preferred_element_type=F32)
        values = jnp.where(live_col, values, 0.0).astype(BF16)
        ones = jnp.where(live_col[0:16, :], 1.0, 0.0).astype(BF16)
        for h in range(heads):
            vt[h, 0:HS, :] = values[h * HS : (h + 1) * HS, :]
            vt[h, HS:, :] = ones

        def score(h):
            pair = (h // 2) * 2 * HS
            return lax.dot_general(
                keys[:, pair : pair + 2 * HS], qm[h], NT, preferred_element_type=F32
            )

        ahead = score(0)
        for h in range(heads):
            scores = ahead
            if h + 1 < heads:
                ahead = score(h + 1)
            old = top[h : h + 1, :]
            new = jnp.maximum(old, jnp.max(scores, axis=0, keepdims=True))
            probs = jnp.exp2(scores - new).astype(BF16)
            top[h : h + 1, :] = new
            acc[h] = acc[h] * jnp.exp2(old - new) + jnp.dot(
                vt[h], probs, preferred_element_type=F32
            )

    on_line(0, 0, True)
    on_line(0, 1, True)
    stream_half[my_rows, :] = own_rows[:, my_cols]
    stream_copy = remote(
        own_rows.at[:, sib_cols], stream_half.at[my_rows], stream_sem.at[0], stream_sem.at[1],
        head=other,
    )
    stream_copy.start()
    for j in range(1, n):
        count_copy(j).wait()
    for ch in range(2):
        sib_arrival(b, ch).wait_recv()
    query = jnp.dot(all_normed[b], wq[...], preferred_element_type=F32) * (
        math.log2(math.e) / HS**0.5
    )
    lane = lax.broadcasted_iota(jnp.int32, (rows, 2 * HS), 1) // HS
    for h in range(heads):
        pair = (h // 2) * 2 * HS
        qm[h] = jnp.where(lane == h % 2, query[:, pair : pair + 2 * HS], 0.0).astype(BF16)

    last = 2 * nz + 1 if lanes_y > 1 else 2 * nz - 1

    def step(s, carry):
        k, ch = s // 2, s % 2

        @pl.when((k > 0) & (k < nz))
        def _():
            on_line(k, ch)

        if lanes_y > 1:

            @pl.when(k > 0)
            def _():
                across(k - 1, ch)

            on_own = (ch == 1) & (k < nz)
            place = jnp.where(on_own, k, jnp.maximum(k - 2 + ch, 0))
            block = line(place) * lanes_y + jnp.where(on_own, yi, lanes_y - 1 - yi)
        else:
            block = line(k)

        @pl.when((s != 2) if lanes_y > 1 else (ch == 1))
        def _():
            @pl.when(s > 1)
            def _():
                for piece_index in range(2):
                    sib_arrival(block, piece_index).wait_recv()

            attend(block)

        return carry

    lax.fori_loop(1, last + 1, step, 0)

    context = []
    for h in range(heads):
        context.append(acc[h, 0:HS, :] / acc[h, HS : HS + 1, :])
    context = jnp.concatenate(context, axis=0).T.astype(BF16)
    sent_out[...] = jnp.dot(context, wo[:, sib_cols], preferred_element_type=F32).astype(BF16)
    out_copy = remote(sent_out, got_out, out_sem.at[0], out_sem.at[1], head=other)
    out_copy.start()
    mine = jnp.dot(context, wo[:, my_cols], preferred_element_type=F32)
    stream_copy.wait()
    mine = mine + stream_half[...].astype(F32)
    out_copy.wait()
    out[...] = (mine + got_out[...].astype(F32)).astype(BF16)

    def drain(s, carry):
        k, ch = s // 2, s % 2
        z = line(k)
        block = z * lanes_y + yi

        @pl.when((z <= zi) & (zi < nz - 1))
        def _():
            z_copy(block, ch, 1).wait_send()

        @pl.when((z >= zi) & (zi > 0))
        def _():
            z_copy(block, ch, 0).wait_send()

        if lanes_y > 1:
            y_copy(block, ch).wait_send()
            sib_copy(z * lanes_y + (lanes_y - 1 - yi), ch).wait_send()
        sib_copy(block, ch).wait_send()
        return carry

    lax.fori_loop(0, 2 * nz, drain, 0)


def local(n, lanes_y, tokens, counts, face_owner, face_row, face_count, mix_w, gain, query_w, key_w, value_w, out_w):
    rows, width = tokens.shape
    half_w = width // 2
    heads = half_w // HS
    nz = n // lanes_y
    any_, vmem = pl.BlockSpec(memory_space=pl.ANY), pl.BlockSpec(memory_space=pltpu.VMEM)
    smem = pl.BlockSpec(memory_space=pltpu.SMEM)
    sem = pltpu.SemaphoreType.DMA
    return pl.pallas_call(
        functools.partial(kernel, n, lanes_y),
        out_shape=jax.ShapeDtypeStruct((rows, half_w), BF16),
        in_specs=[any_, smem, vmem, vmem, vmem, vmem, any_, any_, any_, any_, any_],
        out_specs=vmem,
        scratch_shapes=[
            pltpu.VMEM((3, rows, half_w), BF16),
            pltpu.VMEM((rows // 2, width), BF16),
            pltpu.VMEM((rows, 3 * rows), BF16),
            pltpu.VMEM((128, rows), F32),
            pltpu.VMEM((rows, width), BF16),
            pltpu.VMEM((n, rows, width), BF16),
            pltpu.VMEM((rows, half_w), BF16),
            pltpu.VMEM((n, 8, 128), jnp.int32),
            pltpu.VMEM((width, width), BF16),
            pltpu.VMEM((width, half_w), BF16),
            pltpu.VMEM((width, half_w), BF16),
            pltpu.VMEM((width, half_w), BF16),
            pltpu.VMEM((half_w, width), BF16),
            pltpu.VMEM((half_w, width), BF16),
            pltpu.VMEM((heads, rows, 2 * HS), BF16),
            pltpu.VMEM((heads, HS + 16, rows), BF16),
            pltpu.VMEM((heads, HS + 16, rows), F32),
            pltpu.VMEM((8, rows), F32),
            pltpu.VMEM((rows, half_w), BF16),
            pltpu.VMEM((rows, half_w), BF16),
            sem((7,)), sem((2,)), sem((2,)), sem((2,)), sem((2,)), sem((n,)), sem((n,)),
            sem((2, nz, 2)), sem((nz, 2)), sem((nz, 2)), sem((nz, 2)), sem((n, 2)), sem((n, 2)),
            sem((2,)), sem((2,)),
        ],
        compiler_params=pltpu.CompilerParams(
            collective_id=0, has_side_effects=True, vmem_limit_bytes=60 * 2**20
        ),
    )(
        tokens, counts, face_owner, face_row, face_count[None, :], gain[None, :],
        mix_w, query_w, key_w, value_w, out_w,
    )


def solution(mesh):
    n = mesh.shape["blk"]
    lanes_y = 2 if n == 8 else 1
    rows = P(("sec", "blk"), None)
    in_specs = (
        rows, P(("sec", "blk")), P(None, ("sec", "blk")), P(None, ("sec", "blk")),
        P(("sec", "blk")), P(None, "head"), P(), P(None, "head"), P(None, "head"),
        P(None, "head"), P("head", None),
    )
    return jax.shard_map(
        functools.partial(local, n, lanes_y), mesh=mesh, in_specs=in_specs,
        out_specs=P(("sec", "blk"), "head"), check_vma=False,
    )
```

```python
import functools
import math

import jax
import jax.numpy as jnp
from jax import lax
from jax.experimental import pallas as pl
from jax.experimental.pallas import tpu as pltpu
from jax.sharding import PartitionSpec as P

MESH = pl.DeviceIdType.MESH
HS = 64
NT = (((1,), (1,)), ((), ()))
F32 = jnp.float32
BF16 = jnp.bfloat16


def kernel(
    n, lanes_y,
    tokens, counts, face_owner, face_row, face_count, gain, mix_w, query_w, key_w, value_w, out_w,
    out,
    ext, own_rows, onehot, pack, summed, all_normed, stream_half, count_all,
    mix_full, wq, wk, wv, wvt, wo, qm, vt, acc, top, sent_out, got_out,
    local_sem, halo_send, halo_recv, mix_sem, sum_sem, count_send, count_recv,
    z_send, z_recv, y_send, y_recv, sib_send, sib_recv, stream_sem, out_sem,
):
    rows, width = tokens.shape
    half_w = width // 2
    half_r = rows // 2
    piece = half_r // 2
    heads = half_w // HS
    faces = face_owner.shape[0]
    b = lax.axis_index("blk")
    c = lax.axis_index("head")
    other = 1 - c
    nz = n // lanes_y
    zi, yi = b // lanes_y, b % lanes_y
    my_rows = pl.ds(pl.multiple_of(c * half_r, half_r), half_r)
    sib_rows = pl.ds(pl.multiple_of(other * half_r, half_r), half_r)
    my_cols = pl.ds(pl.multiple_of(c * half_w, 128), half_w)
    sib_cols = pl.ds(pl.multiple_of(other * half_w, 128), half_w)

    def remote(src, dst, send, recv, **where):
        return pltpu.make_async_remote_copy(
            src_ref=src, dst_ref=dst, send_sem=send, recv_sem=recv,
            device_id=where, device_id_type=MESH,
        )

    loads = [
        pltpu.make_async_copy(tokens.at[:, my_cols], ext.at[1], local_sem.at[0]),
        pltpu.make_async_copy(tokens.at[my_rows, :], own_rows, local_sem.at[1]),
        pltpu.make_async_copy(mix_w, mix_full.at[:, my_cols], local_sem.at[2]),
        pltpu.make_async_copy(query_w, wq, local_sem.at[3]),
        pltpu.make_async_copy(key_w, wk, local_sem.at[4]),
        pltpu.make_async_copy(value_w, wv, local_sem.at[5]),
        pltpu.make_async_copy(out_w, wo, local_sem.at[6]),
    ]

    barrier = pltpu.get_barrier_semaphore()
    for j in range(1, n):
        pl.semaphore_signal(barrier, inc=1, device_id={"blk": (b + j) % n}, device_id_type=MESH)
    pl.semaphore_signal(barrier, inc=1, device_id={"head": other}, device_id_type=MESH)
    pl.semaphore_wait(barrier, n)

    up, down = (b + 1) % n, (b + n - 1) % n
    halo_up = remote(tokens.at[:, my_cols], ext.at[0], halo_send.at[0], halo_recv.at[0], blk=up)
    halo_down = remote(tokens.at[:, my_cols], ext.at[2], halo_send.at[1], halo_recv.at[1], blk=down)
    halo_up.start()
    halo_down.start()
    mix_copy = remote(mix_w, mix_full.at[:, my_cols], mix_sem.at[0], mix_sem.at[1], head=other)
    mix_copy.start()
    for load in loads:
        load.start()

    count_all[b] = jnp.full((8, 128), counts[0], jnp.int32)

    def count_copy(j):
        return remote(
            count_all.at[b], count_all.at[b], count_send.at[j], count_recv.at[j], blk=(b + j) % n
        )

    for j in range(1, n):
        count_copy(j).start()

    off = face_owner[...] - b + 1
    off = jnp.where(off < 0, off + n, off)
    off = jnp.where(off >= n, off - n, off)
    index = off * rows + face_row[...]
    face = lax.broadcasted_iota(jnp.int32, (faces, rows), 0)
    index = jnp.where(face < face_count[...], index, -1)
    pack[...] = jnp.zeros_like(pack)
    pack[0:faces, :] = index.astype(F32)
    pack[faces : faces + 1, :] = face_count[...].astype(F32)
    pack_t = pack[...].T
    face_total = pack_t[:, faces : faces + 1]
    for s in range(3):
        place = (lax.broadcasted_iota(jnp.int32, (rows, rows), 1) + s * rows).astype(F32)
        total = jnp.zeros((rows, rows), F32)
        for f in range(faces):
            total = total + jnp.where(pack_t[:, f : f + 1] == place, 1.0, 0.0)
        onehot[:, s * rows : (s + 1) * rows] = total.astype(BF16)

    for load in loads:
        load.wait()
    wvt[...] = wv[...].astype(F32).T.astype(BF16)
    acc[...] = jnp.zeros_like(acc)
    top[...] = jnp.full_like(top, -1e30)

    part = jnp.dot(onehot[:, rows : 2 * rows], ext[1], preferred_element_type=F32)
    halo_up.wait()
    part += jnp.dot(onehot[:, 0:rows], ext[0], preferred_element_type=F32)
    halo_down.wait()
    part += jnp.dot(onehot[:, 2 * rows :], ext[2], preferred_element_type=F32)
    summed[:, my_cols] = (part / face_total).astype(BF16)
    sum_copy = remote(
        summed.at[sib_rows, my_cols], summed.at[sib_rows, my_cols], sum_sem.at[0], sum_sem.at[1],
        head=other,
    )
    sum_copy.start()
    mix_copy.wait()
    sum_copy.wait()
    def finish(ch):
        stream = own_rows[ch * piece : (ch + 1) * piece, :].astype(F32) + jnp.dot(
            summed[pl.ds(pl.multiple_of(c * half_r + ch * piece, piece), piece), :],
            mix_full[...], preferred_element_type=F32,
        )
        own_rows[ch * piece : (ch + 1) * piece, :] = stream.astype(BF16)
        stream = own_rows[ch * piece : (ch + 1) * piece, :].astype(F32)
        var = jnp.mean(stream * stream, axis=-1, keepdims=True)
        all_normed[b, pl.ds(pl.multiple_of(c * half_r + ch * piece, piece), piece), :] = (
            stream * lax.rsqrt(var + 1e-05) * gain[...].astype(F32)
        ).astype(BF16)

    def chunk(block, ch):
        return all_normed.at[block, pl.ds(pl.multiple_of(c * half_r + ch * piece, piece), piece)]

    def z_copy(block, ch, direction):
        step = 2 * direction - 1
        return remote(
            chunk(block, ch), chunk(block, ch), z_send.at[direction, block // lanes_y, ch],
            z_recv.at[block // lanes_y, ch], blk=b + step * lanes_y,
        )

    def y_copy(block, ch):
        return remote(
            chunk(block, ch), chunk(block, ch), y_send.at[block // lanes_y, ch],
            y_recv.at[block // lanes_y, ch], blk=zi * lanes_y + (lanes_y - 1 - yi),
        )

    def sib_copy(block, ch):
        return remote(
            chunk(block, ch), chunk(block, ch), sib_send.at[block, ch], sib_recv.at[block, ch],
            head=other,
        )

    def sib_arrival(block, ch):
        place = pl.ds(pl.multiple_of(other * half_r + ch * piece, piece), piece)
        return remote(
            all_normed.at[block, place], all_normed.at[block, place],
            sib_send.at[block, ch], sib_recv.at[block, ch], head=other,
        )

    near = jnp.minimum(zi, nz - 1 - zi)
    far_sign = jnp.where(zi < nz - 1 - zi, 1, -1)

    def line(k):
        close = zi + (1 - 2 * (k % 2)) * ((k + 1) // 2)
        return jnp.where(k <= 2 * near, close, zi + far_sign * (k - near))

    def on_line(k, ch, first=False):
        z = line(k)
        block = z * lanes_y + yi
        if not first:
            z_copy(block, ch, 1).wait_recv()

        if lanes_y > 1:
            y_copy(block, ch).start()

        @pl.when((z <= zi) & (zi < nz - 1))
        def _():
            z_copy(block, ch, 1).start()

        @pl.when((z >= zi) & (zi > 0))
        def _():
            z_copy(block, ch, 0).start()

        sib_copy(block, ch).start()

    def across(k, ch):
        block = line(k) * lanes_y + (lanes_y - 1 - yi)
        y_copy(block, ch).wait_recv()
        sib_copy(block, ch).start()

    def attend(block):
        live = count_all[block]
        normed = all_normed[block]
        live_row = lax.broadcasted_iota(jnp.int32, (rows, half_w), 0) < live[0:1, 0:1]
        keys = jnp.dot(normed, wk[...], preferred_element_type=F32)
        keys = jnp.where(live_row, keys, keys[0:1, :]).astype(BF16)
        live_col = lax.broadcasted_iota(jnp.int32, (half_w, rows), 1) < live[0:1, 0:1]
        values = lax.dot_general(wvt[...], normed, NT, preferred_element_type=F32)
        values = jnp.where(live_col, values, 0.0).astype(BF16)
        ones = jnp.where(live_col[0:16, :], 1.0, 0.0).astype(BF16)
        for h in range(heads):
            vt[h, 0:HS, :] = values[h * HS : (h + 1) * HS, :]
            vt[h, HS:, :] = ones

        def score(h):
            pair = (h // 2) * 2 * HS
            return lax.dot_general(
                keys[:, pair : pair + 2 * HS], qm[h], NT, preferred_element_type=F32
            )

        ahead = score(0)
        for h in range(heads):
            scores = ahead
            if h + 1 < heads:
                ahead = score(h + 1)
            old = top[h : h + 1, :]
            new = jnp.maximum(old, jnp.max(scores, axis=0, keepdims=True))
            probs = jnp.exp2(scores - new).astype(BF16)
            top[h : h + 1, :] = new
            acc[h] = acc[h] * jnp.exp2(old - new) + jnp.dot(
                vt[h], probs, preferred_element_type=F32
            )

    finish(0)
    on_line(0, 0, True)
    finish(1)
    on_line(0, 1, True)
    stream_half[my_rows, :] = own_rows[:, my_cols]
    stream_copy = remote(
        own_rows.at[:, sib_cols], stream_half.at[my_rows], stream_sem.at[0], stream_sem.at[1],
        head=other,
    )
    stream_copy.start()
    for j in range(1, n):
        count_copy(j).wait()
    for ch in range(2):
        sib_arrival(b, ch).wait_recv()
    query = jnp.dot(all_normed[b], wq[...], preferred_element_type=F32) * (
        math.log2(math.e) / HS**0.5
    )
    lane = lax.broadcasted_iota(jnp.int32, (rows, 2 * HS), 1) // HS
    for h in range(heads):
        pair = (h // 2) * 2 * HS
        qm[h] = jnp.where(lane == h % 2, query[:, pair : pair + 2 * HS], 0.0).astype(BF16)

    last = 2 * nz + 1 if lanes_y > 1 else 2 * nz - 1

    def step(s, carry):
        k, ch = s // 2, s % 2

        @pl.when((k > 0) & (k < nz))
        def _():
            on_line(k, ch)

        if lanes_y > 1:

            @pl.when(k > 0)
            def _():
                across(k - 1, ch)

            on_own = (ch == 1) & (k < nz)
            place = jnp.where(on_own, k, jnp.maximum(k - 2 + ch, 0))
            block = line(place) * lanes_y + jnp.where(on_own, yi, lanes_y - 1 - yi)
        else:
            block = line(k)

        @pl.when((s != 2) if lanes_y > 1 else (ch == 1))
        def _():
            @pl.when(s > 1)
            def _():
                for piece_index in range(2):
                    sib_arrival(block, piece_index).wait_recv()

            attend(block)

        return carry

    lax.fori_loop(1, last + 1, step, 0)

    context = []
    for h in range(heads):
        context.append(acc[h, 0:HS, :] / acc[h, HS : HS + 1, :])
    context = jnp.concatenate(context, axis=0).T.astype(BF16)
    sent_out[...] = jnp.dot(context, wo[:, sib_cols], preferred_element_type=F32).astype(BF16)
    out_copy = remote(sent_out, got_out, out_sem.at[0], out_sem.at[1], head=other)
    out_copy.start()
    mine = jnp.dot(context, wo[:, my_cols], preferred_element_type=F32)
    stream_copy.wait()
    mine = mine + stream_half[...].astype(F32)
    out_copy.wait()
    out[...] = (mine + got_out[...].astype(F32)).astype(BF16)

    def drain(s, carry):
        k, ch = s // 2, s % 2
        z = line(k)
        block = z * lanes_y + yi

        @pl.when((z <= zi) & (zi < nz - 1))
        def _():
            z_copy(block, ch, 1).wait_send()

        @pl.when((z >= zi) & (zi > 0))
        def _():
            z_copy(block, ch, 0).wait_send()

        if lanes_y > 1:
            y_copy(block, ch).wait_send()
            sib_copy(z * lanes_y + (lanes_y - 1 - yi), ch).wait_send()
        sib_copy(block, ch).wait_send()
        return carry

    lax.fori_loop(0, 2 * nz, drain, 0)


def local(n, lanes_y, tokens, counts, face_owner, face_row, face_count, mix_w, gain, query_w, key_w, value_w, out_w):
    rows, width = tokens.shape
    half_w = width // 2
    heads = half_w // HS
    nz = n // lanes_y
    any_, vmem = pl.BlockSpec(memory_space=pl.ANY), pl.BlockSpec(memory_space=pltpu.VMEM)
    smem = pl.BlockSpec(memory_space=pltpu.SMEM)
    sem = pltpu.SemaphoreType.DMA
    return pl.pallas_call(
        functools.partial(kernel, n, lanes_y),
        out_shape=jax.ShapeDtypeStruct((rows, half_w), BF16),
        in_specs=[any_, smem, vmem, vmem, vmem, vmem, any_, any_, any_, any_, any_],
        out_specs=vmem,
        scratch_shapes=[
            pltpu.VMEM((3, rows, half_w), BF16),
            pltpu.VMEM((rows // 2, width), BF16),
            pltpu.VMEM((rows, 3 * rows), BF16),
            pltpu.VMEM((128, rows), F32),
            pltpu.VMEM((rows, width), BF16),
            pltpu.VMEM((n, rows, width), BF16),
            pltpu.VMEM((rows, half_w), BF16),
            pltpu.VMEM((n, 8, 128), jnp.int32),
            pltpu.VMEM((width, width), BF16),
            pltpu.VMEM((width, half_w), BF16),
            pltpu.VMEM((width, half_w), BF16),
            pltpu.VMEM((width, half_w), BF16),
            pltpu.VMEM((half_w, width), BF16),
            pltpu.VMEM((half_w, width), BF16),
            pltpu.VMEM((heads, rows, 2 * HS), BF16),
            pltpu.VMEM((heads, HS + 16, rows), BF16),
            pltpu.VMEM((heads, HS + 16, rows), F32),
            pltpu.VMEM((8, rows), F32),
            pltpu.VMEM((rows, half_w), BF16),
            pltpu.VMEM((rows, half_w), BF16),
            sem((7,)), sem((2,)), sem((2,)), sem((2,)), sem((2,)), sem((n,)), sem((n,)),
            sem((2, nz, 2)), sem((nz, 2)), sem((nz, 2)), sem((nz, 2)), sem((n, 2)), sem((n, 2)),
            sem((2,)), sem((2,)),
        ],
        compiler_params=pltpu.CompilerParams(
            collective_id=0, has_side_effects=True, vmem_limit_bytes=60 * 2**20
        ),
    )(
        tokens, counts, face_owner, face_row, face_count[None, :], gain[None, :],
        mix_w, query_w, key_w, value_w, out_w,
    )


def solution(mesh):
    n = mesh.shape["blk"]
    lanes_y = 2 if n == 8 else 1
    rows = P(("sec", "blk"), None)
    in_specs = (
        rows, P(("sec", "blk")), P(None, ("sec", "blk")), P(None, ("sec", "blk")),
        P(("sec", "blk")), P(None, "head"), P(), P(None, "head"), P(None, "head"),
        P(None, "head"), P("head", None),
    )
    return jax.shard_map(
        functools.partial(local, n, lanes_y), mesh=mesh, in_specs=in_specs,
        out_specs=P(("sec", "blk"), "head"), check_vma=False,
    )
```
